32 devices in a mesh: dp: 2 (over x), row: 4 (over y, core), col: 4 (over z).
Axes of the slice: x: 2, y: 2, z: 4, core: 2. Of those that a mesh axis runs over, the one named last changes fastest.
Arguments:
- inputs: float32 [4096, 1088], P(('dp', 'row')), may hold values from -6 to 6
- segment_ids: int32 [4096], P(('dp', 'row')), may hold values from 0 to 2, as said below
- head_map: int32 [17], replicated, may hold values from 0 to 31, as said below
- gain_one: float32 [2, 1088], replicated, may hold values from 0.5 to 1.5
- shift_one: float32 [2, 1088], replicated, may hold values from -1.2 to 1.2
- gain_two: float32 [2, 1088], replicated, may hold values from 0.5 to 1.5
- shift_two: float32 [2, 1088], replicated, may hold values from -1.2 to 1.2
- w_qkv: bfloat16 [2, 1088, 6144], P(None, 'row', 'col'), may hold values from -0.1875 to 0.1875
- w_out: bfloat16 [2, 2048, 1088], P(None, 'col', 'row'), may hold values from -1.5 to 1.5
- w_up: bfloat16 [2, 1088, 4352], P(None, 'row', 'col'), may hold values from -0.1875 to 0.1875
- w_down: bfloat16 [2, 4352, 1088], P(None, 'col', 'row'), may hold values from -0.09375 to 0.09375
- cotangent: float32 [4096, 1088], P(('dp', 'row')), may hold values from -6 to 6
Outputs:
- output: float32 [4096, 1088], P(('dp', 'row'))
- grad_inputs: float32 [4096, 1088], P(('dp', 'row'))
- grad_gain_one: float32 [2, 1088], replicated
- grad_shift_one: float32 [2, 1088], replicated
- grad_gain_two: float32 [2, 1088], replicated
- grad_shift_two: float32 [2, 1088], replicated
- grad_qkv: float32 [2, 1088, 6144], P(None, 'row', 'col')
- grad_out: float32 [2, 2048, 1088], P(None, 'col', 'row')
- grad_up: float32 [2, 1088, 4352], P(None, 'row', 'col')
- grad_down: float32 [2, 4352, 1088], P(None, 'col', 'row')
The draws below stay inside these ranges and needn't reach their ends.
Inputs may be any that keep to these rules, and one draw needn't show every extreme that they name: `segment_ids`: within each sequence of 2048 tokens the ids are 0, 1, 2 in order, never falling; document 1 starts before token 512 and ends after token 1536 of its sequence. `head_map`: the heads use distinct slots; slot s lies on index s // 8 of col; each index of col holds at most 8 heads, and one holds exactly 8.
All inputs are finite; a program needn't handle non-finite values.
Results may differ from the reference program's by a relative error of at most 0.023.
Values may be sent and summed in bfloat16 or wider, within the bound.
A program may use at most 256 MiB of HBM per device.

```python
import jax
import jax.numpy as jnp
from jax import lax

D = 1088
HEADS = 17
HD = 64
FF = 4352
SLOT_DEV = 8
LAYERS = 2
ROW_TOK = 512
SEQ = 2048
SLOTS = 32
TOKENS = 4096
N_DP = 2
N_ROW = 4
N_COL = 4


def draw_segment_ids(key, part):
    key = jax.random.fold_in(key, 11)
    first_key, second_key = jax.random.split(key)
    starts = jax.random.randint(first_key, (N_DP, 1), SEQ // 16, SEQ // 4)
    finish = jax.random.randint(second_key, (N_DP, 1), SEQ - SEQ // 4 + 1, SEQ - SEQ // 16 + 1)
    places = jnp.arange(SEQ, dtype=jnp.int32)[None, :]
    labels = (places >= starts).astype(jnp.int32) + (places >= finish).astype(jnp.int32)
    return labels.reshape(TOKENS)


def draw_head_map(key, part):
    key = jax.random.fold_in(key, 23)
    pick_key, order_key, deal_key = jax.random.split(key, 3)
    full_device = jax.random.randint(pick_key, (), 0, N_COL)
    slot_ids = jnp.arange(SLOTS, dtype=jnp.int32)
    ranking = jax.random.permutation(order_key, SLOTS).astype(jnp.int32)
    forced = (slot_ids // SLOT_DEV == full_device) | (slot_ids == 0) | (slot_ids == SLOTS - 1)
    ranking = ranking - jnp.where(forced, SLOTS, 0).astype(jnp.int32)
    chosen = jnp.argsort(ranking, stable=True)[:HEADS].astype(jnp.int32)
    return chosen[jax.random.permutation(deal_key, HEADS)]


def block_scale(own_key, shape, cuts, smallest, largest):
    level, own = 1.0, jax.random.fold_in(own_key, 6)
    for position, parts in cuts:
        draws = jnp.exp(jax.random.uniform(jax.random.fold_in(own, position), (parts,), jnp.float32, smallest / len(cuts), largest / len(cuts)))
        level = level * jnp.repeat(draws, shape[position] // parts).reshape([-1 if axis == position else 1 for axis in range(len(shape))])
    return level


def scatter_about(stream_key, shape, scale, limit, shards=(), kind=jnp.bfloat16):
    entries = scale * jax.random.normal(stream_key, shape, jnp.float32)
    if shards:
        entries = entries * block_scale(stream_key, shape, shards, -0.22, 0.18)
    return jnp.clip(entries, -limit, limit).astype(kind)


def setup_inputs(seed: int = 0) -> dict:
    key_list = jax.random.split(jax.random.key(seed), 13)
    inputs = scatter_about(key_list[0], (TOKENS, D), 1.0, 6.0, ((0, 8),), jnp.float32)
    segment_ids = draw_segment_ids(jax.random.fold_in(key_list[12], 71), 0)
    head_map = draw_head_map(jax.random.fold_in(key_list[12], 71), 0)
    gain_one = jnp.clip(1.0 + 0.1 * jax.random.normal(key_list[3], (LAYERS, D), jnp.float32), 0.5, 1.5)
    shift_one = scatter_about(key_list[4], (LAYERS, D), 0.2, 1.2, (), jnp.float32)
    gain_two = jnp.clip(1.0 + 0.1 * jax.random.normal(key_list[5], (LAYERS, D), jnp.float32), 0.5, 1.5)
    shift_two = scatter_about(key_list[6], (LAYERS, D), 0.2, 1.2, (), jnp.float32)
    w_qkv = scatter_about(key_list[7], (LAYERS, D, SLOTS * 3 * HD), D ** -0.5, 0.1875, ((1, 4), (2, 4)))
    w_out = scatter_about(key_list[8], (LAYERS, SLOTS * HD, D), (D // 64) ** -0.5, 1.5, ((1, 4), (2, 4)))
    w_up = scatter_about(key_list[9], (LAYERS, D, FF), D ** -0.5, 0.1875, ((1, 4), (2, 4)))
    w_down = scatter_about(key_list[10], (LAYERS, FF, D), FF ** -0.5, 0.09375, ((1, 4), (2, 4)))
    cotangent = scatter_about(key_list[11], (TOKENS, D), 1.0, 6.0, ((0, 8),), jnp.float32)
    return dict(inputs=inputs, segment_ids=segment_ids, head_map=head_map, gain_one=gain_one, shift_one=shift_one, gain_two=gain_two, shift_two=shift_two, w_qkv=w_qkv, w_out=w_out, w_up=w_up, w_down=w_down, cotangent=cotangent)


@jax.custom_vjp
def low(v):
    return lax.optimization_barrier(v.astype(jnp.bfloat16)).astype(jnp.float32)

@jax.custom_vjp
def low_back(v):
    return v

def low_keep(v):
    return (low(v), None)

def low_pass(kept, grad):
    return (grad,)

def back_keep(v):
    return (v, None)

def back_low(kept, grad):
    return (low(grad),)
low.defvjp(low_keep, low_pass)
low_back.defvjp(back_keep, back_low)
norm_eps = 1e-05
masked_score = -1e+30
highest = lax.Precision.HIGHEST

def layer_norm(stream, scales, shifts):
    centre = stream - lax.optimization_barrier(jnp.mean(stream, axis=-1, keepdims=True))
    inverse = lax.rsqrt(lax.optimization_barrier(jnp.mean(centre * centre, axis=-1, keepdims=True)) + norm_eps)
    return centre * inverse * scales + shifts

def attend_rows(index, queries, key_part, value_part, segment):
    begin = index * ROW_TOK
    block_query = lax.dynamic_slice_in_dim(queries, begin, ROW_TOK, 0)
    block_segment = lax.dynamic_slice_in_dim(segment, begin, ROW_TOK, 0)
    logits = low_back(jnp.einsum('qhd,khd->hqk', block_query, key_part, precision=highest)) * HD ** (-0.5)
    query_pos = begin + jnp.arange(ROW_TOK, dtype=jnp.int32)
    key_pos = jnp.arange(SEQ, dtype=jnp.int32)
    allowed = (key_pos[None, :] <= query_pos[:, None]) & (segment[None, :] == block_segment[:, None])
    logits = jnp.where(allowed[None], logits, masked_score)
    highest_score = lax.optimization_barrier(jnp.max(logits, axis=-1, keepdims=True))
    weights = jnp.exp(logits - highest_score)
    weights = weights / lax.optimization_barrier(jnp.sum(weights, axis=-1, keepdims=True))
    return jnp.einsum('hqk,khd->qhd', low(weights), value_part, precision=highest)

def attention(queries, key_part, value_part, segment):

    def one_block(index):
        return attend_rows(index, queries, key_part, value_part, segment)
    blocks = lax.map(jax.checkpoint(one_block), jnp.arange(N_ROW, dtype=jnp.int32))
    return blocks.reshape(SEQ, HEADS, HD)

def run_layers(stream, segment, head_map, params):
    gain_one, shift_one, gain_two, shift_two, w_qkv, w_out, w_up, w_down = params
    for layer in range(LAYERS):
        normed = low(layer_norm(stream, gain_one[layer], shift_one[layer]))
        packed = w_qkv[layer].reshape(D, SLOTS, 3 * HD)[:, head_map, :]
        mixed = low(low_back(jnp.einsum('td,dhe->the', normed, packed, precision=highest)))
        heads = attention(mixed[..., :HD], mixed[..., HD:2 * HD], mixed[..., 2 * HD:], segment)
        heads = low(low_back(heads))
        rows_out = w_out[layer].reshape(SLOTS, HD, D)[head_map]
        stream = stream + low_back(jnp.einsum('thd,hde->te', heads, rows_out, precision=highest))
        normed = low(layer_norm(stream, gain_two[layer], shift_two[layer]))
        hidden = low_back(jnp.dot(normed, w_up[layer], precision=highest))
        active = low(jax.nn.gelu(hidden, approximate=False))
        stream = stream + low_back(jnp.dot(active, w_down[layer], precision=highest))
    return stream

def reference(inputs, segment_ids, head_map, gain_one, shift_one, gain_two, shift_two, w_qkv, w_out, w_up, w_down, cotangent):
    params = (gain_one, shift_one, gain_two, shift_two, w_qkv.astype(jnp.float32), w_out.astype(jnp.float32), w_up.astype(jnp.float32), w_down.astype(jnp.float32))
    stream_seq = inputs.reshape(N_DP, SEQ, D)
    segment_seq = segment_ids.reshape(N_DP, SEQ)
    grad_seq = cotangent.reshape(N_DP, SEQ, D)

    def per_sequence(totals, pieces):
        stream, segment, grad_result = pieces

        def forward(stream_in, weights):
            return run_layers(stream_in, segment, head_map, weights)
        result, pullback = jax.vjp(forward, stream, params)
        grad_stream, grad_params = pullback(grad_result)
        totals = jax.tree.map(jnp.add, totals, grad_params)
        return (totals, (result, grad_stream))
    zeros_start = jax.tree.map(jnp.zeros_like, params)
    totals, outcome = lax.scan(per_sequence, zeros_start, (stream_seq, segment_seq, grad_seq))
    results, grads_in = outcome
    return (results.reshape(TOKENS, D), grads_in.reshape(TOKENS, D), totals[0], totals[1], totals[2], totals[3], totals[4], totals[5], totals[6], totals[7])
```

```python
from functools import partial

import jax
import jax.numpy as jnp
from jax import lax
from jax.experimental import pallas as pl
from jax.experimental.pallas import tpu as pltpu
from jax.sharding import PartitionSpec as P

HD = 64
LAYERS = 2


norm_eps = 1e-05
masked_score = -1e30
start_score = -1e20


def norm_forward(stream, scales, shifts):
    centre = stream - jnp.mean(stream, axis=-1, keepdims=True)
    inverse = lax.rsqrt(jnp.mean(centre * centre, axis=-1, keepdims=True) + norm_eps)
    standard = centre * inverse
    return (standard * scales + shifts, standard, inverse)


def norm_backward(incoming, standard, inverse, scales):
    scaled = incoming * scales
    grad_stream = inverse * (
        scaled
        - jnp.mean(scaled, axis=-1, keepdims=True)
        - standard * jnp.mean(scaled * standard, axis=-1, keepdims=True)
    )
    return (grad_stream, jnp.sum(incoming * standard, axis=0), jnp.sum(incoming, axis=0))


def swap(value, axis, bit):
    count = lax.axis_size(axis)
    return lax.ppermute(value, axis, [(i, i ^ bit) for i in range(count)])


def gather_rows(shard):
    count = lax.axis_size("row")
    me = lax.axis_index("row")
    held = shard
    bit, done = count // 2, 0
    while bit:
        other = swap(held, "row", bit)
        upper = (me & bit) != 0
        held = jnp.stack(
            [jnp.where(upper, other, held), jnp.where(upper, held, other)], axis=done
        )
        bit, done = bit // 2, done + 1
    return held.reshape((count * shard.shape[0],) + shard.shape[1:])


def everyone_sum(pieces):
    for axis in ("row", "dp"):
        bit = 1
        while bit < lax.axis_size(axis):
            pieces = pieces + swap(pieces, axis, bit)
            bit *= 2
    return pieces


def column_sum(pieces):
    return lax.psum(pieces.astype(jnp.bfloat16), "col").astype(jnp.float32)


def contract_rows(left, right):
    return lax.dot_general(
        left, right, (((0,), (0,)), ((), ())), preferred_element_type=jnp.float32
    )


def contract_cols(left, right):
    return lax.dot_general(
        left, right, (((1,), (1,)), ((), ())), preferred_element_type=jnp.float32
    )


class Share:
    def __init__(self, left, right, right_dim=0):
        row_count = lax.axis_size("row")
        tokens_here, width = left.shape
        self.piece = width // row_count

        def product(part):
            return lax.dot_general(
                part, right, (((0,), (right_dim,)), ((), ())), preferred_element_type=jnp.float32
            )

        halves = left.reshape(tokens_here, row_count // 2, 2, self.piece)
        even = halves[:, :, 0].reshape(tokens_here, width // 2)
        odd = halves[:, :, 1].reshape(tokens_here, width // 2)
        upper = (lax.axis_index("row") & 1) != 0
        self.give = product(jnp.where(upper, even, odd)).astype(jnp.bfloat16)
        self.total = product(jnp.where(upper, odd, even))
        self.steps = [("row", 1 << i) for i in range((row_count - 1).bit_length())]
        self.steps += [("dp", 1 << i) for i in range((lax.axis_size("dp") - 1).bit_length())]

    def begin(self):
        axis, bit = self.steps.pop(0)
        return swap(self.give, axis, bit)

    def finish(self, sent):
        total = self.total + sent.astype(jnp.float32)
        if self.steps and self.steps[0][0] == "row":
            total = total.reshape(-1, 2, self.piece, total.shape[-1])
            upper = (lax.axis_index("row") & self.steps[0][1]) != 0
            self.give = jnp.where(upper, total[:, 0], total[:, 1]).astype(jnp.bfloat16)
            self.give = self.give.reshape(-1, total.shape[-1])
            total = jnp.where(upper, total[:, 1], total[:, 0])
            total = total.reshape(-1, total.shape[-1])
        elif self.steps:
            self.give = total.astype(jnp.bfloat16)
            total = self.give.astype(jnp.float32)
        self.total = total

    def result(self):
        while self.steps:
            self.finish(self.begin())
        return self.total


def beside(value, *shares):
    shares = [share for share in shares if share.steps]
    sent = [share.begin() for share in shares]
    value, *sent = lax.optimization_barrier((value, *sent))
    for share, part in zip(shares, sent):
        share.finish(part)
    return value


def kept(block, tokens_here, low_edge, query_pos):
    key_pos = block * tokens_here + lax.broadcasted_iota(jnp.int32, (tokens_here, tokens_here), 0)
    return (key_pos >= low_edge) & (key_pos <= query_pos)


def attend_kernel(place, used, edge, query, pairs, out, out_low, log_total):
    tokens_here = query.shape[0]
    head_dim = out.shape[0]
    row = place[0]
    queries = query[...]
    low_edge = edge[...]
    query_pos = row * tokens_here + lax.broadcasted_iota(jnp.int32, (1, tokens_here), 1)

    def step(block, state):
        running, denominator, weighted = state
        part = pairs[pl.ds(pl.multiple_of(block * tokens_here, tokens_here), tokens_here), :]
        logits = contract_cols(part, queries)
        logits = jnp.where(
            kept(block, tokens_here, low_edge, query_pos), logits, masked_score
        )
        newest = jnp.maximum(running, jnp.max(logits, axis=0, keepdims=True))
        factor = jnp.exp(running - newest)
        weights = jnp.exp(logits - newest)
        denominator = denominator * factor + jnp.sum(weights, axis=0, keepdims=True)
        weighted = weighted * factor + contract_rows(part, weights.astype(jnp.bfloat16))
        return (newest, denominator, weighted)

    running, denominator, weighted = lax.fori_loop(
        0,
        row + 1,
        step,
        (
            jnp.full((1, tokens_here), start_score, jnp.float32),
            jnp.zeros((1, tokens_here), jnp.float32),
            jnp.zeros((2 * head_dim, tokens_here), jnp.float32),
        ),
    )
    scale = used[pl.program_id(0)].astype(jnp.float32) / denominator
    result = weighted[head_dim:] * scale
    out[...] = result
    out_low[...] = result.astype(jnp.bfloat16)
    log_total[...] = running + jnp.log(denominator)


def back_kernel(place, edge, query, grads, pairs, out, log_total, grad_query, grad_pairs):
    tokens_here = query.shape[0]
    head_dim = out.shape[0]
    row = place[0]
    queries = query[...]
    grad_heads = grads[...]
    low_edge = edge[...]
    logs = log_total[...]
    query_pos = row * tokens_here + lax.broadcasted_iota(jnp.int32, (1, tokens_here), 1)
    turned = grad_heads.astype(jnp.float32).T
    delta = jnp.sum(turned[head_dim:] * out[...], axis=0, keepdims=True)

    def step(block, total):
        here = pl.ds(pl.multiple_of(block * tokens_here, tokens_here), tokens_here)
        part = pairs[here, :]
        logits = contract_cols(part, queries)
        logits = jnp.where(
            kept(block, tokens_here, low_edge, query_pos), logits, masked_score
        )
        weights = jnp.exp(logits - logs)
        grad_weights = contract_cols(part, grad_heads)
        grad_logits = (weights * (grad_weights - delta)).astype(jnp.bfloat16)
        grad_pairs[here, :] = (
            jnp.dot(grad_logits, queries, preferred_element_type=jnp.float32)
            + jnp.dot(
                weights.astype(jnp.bfloat16), grad_heads, preferred_element_type=jnp.float32
            )
        ).astype(jnp.bfloat16)
        return total + contract_rows(part, grad_logits)

    total = lax.fori_loop(
        0, row + 1, step, jnp.zeros((2 * head_dim, tokens_here), jnp.float32)
    )
    grad_query[...] = (total.T * head_dim ** (-0.5)).astype(jnp.bfloat16)

    def clear(block, carry):
        here = pl.ds(pl.multiple_of(block * tokens_here, tokens_here), tokens_here)
        grad_pairs[here, :] = jnp.zeros((tokens_here, 2 * head_dim), jnp.bfloat16)
        return carry

    lax.fori_loop(row + 1, pairs.shape[0] // tokens_here, clear, 0)


def attend(place, used, edge, query, pairs):
    tokens_here, wide = query.shape
    slots = wide // (2 * HD)
    count = pairs.shape[0]
    scalar = pl.BlockSpec(memory_space=pltpu.SMEM)
    return pl.pallas_call(
        attend_kernel,
        grid=(slots,),
        in_specs=[
            scalar,
            scalar,
            pl.BlockSpec((1, tokens_here), lambda s: (0, 0)),
            pl.BlockSpec((tokens_here, 2 * HD), lambda s: (0, s)),
            pl.BlockSpec((count, 2 * HD), lambda s: (0, s)),
        ],
        out_specs=[
            pl.BlockSpec((None, HD, tokens_here), lambda s: (s, 0, 0)),
            pl.BlockSpec((None, HD, tokens_here), lambda s: (s, 0, 0)),
            pl.BlockSpec((None, 1, tokens_here), lambda s: (s, 0, 0)),
        ],
        out_shape=[
            jax.ShapeDtypeStruct((slots, HD, tokens_here), jnp.float32),
            jax.ShapeDtypeStruct((slots, HD, tokens_here), jnp.bfloat16),
            jax.ShapeDtypeStruct((slots, 1, tokens_here), jnp.float32),
        ],
        compiler_params=pltpu.CompilerParams(vmem_limit_bytes=32 * 1024 * 1024),
        cost_estimate=pl.CostEstimate(
            flops=8 * slots * tokens_here * count * 4 * HD,
            bytes_accessed=4 * pairs.size,
            transcendentals=slots * tokens_here * count,
        ),
    )(place, used, edge, query, pairs)


def attend_back(place, edge, query, grads, pairs, out, log_total):
    tokens_here, wide = query.shape
    slots = wide // (2 * HD)
    count = pairs.shape[0]
    scalar = pl.BlockSpec(memory_space=pltpu.SMEM)
    own = pl.BlockSpec((tokens_here, 2 * HD), lambda s: (0, s))
    every = pl.BlockSpec((count, 2 * HD), lambda s: (0, s))
    return pl.pallas_call(
        back_kernel,
        grid=(slots,),
        in_specs=[
            scalar,
            pl.BlockSpec((1, tokens_here), lambda s: (0, 0)),
            own,
            own,
            every,
            pl.BlockSpec((None, HD, tokens_here), lambda s: (s, 0, 0)),
            pl.BlockSpec((None, 1, tokens_here), lambda s: (s, 0, 0)),
        ],
        out_specs=[own, every],
        out_shape=[
            jax.ShapeDtypeStruct(query.shape, jnp.bfloat16),
            jax.ShapeDtypeStruct(pairs.shape, jnp.bfloat16),
        ],
        compiler_params=pltpu.CompilerParams(vmem_limit_bytes=32 * 1024 * 1024),
        cost_estimate=pl.CostEstimate(
            flops=16 * slots * tokens_here * count * 4 * HD,
            bytes_accessed=6 * pairs.size,
            transcendentals=slots * tokens_here * count,
        ),
    )(place, edge, query, grads, pairs, out, log_total)


def body(
    inputs,
    segment_ids,
    head_map,
    gain_one,
    shift_one,
    gain_two,
    shift_two,
    w_qkv,
    w_out,
    w_up,
    w_down,
    cotangent,
):
    row_tokens = inputs.shape[0]
    slot_count = w_out.shape[1] // HD
    slot_ids = lax.axis_index("col") * slot_count + jnp.arange(slot_count, dtype=jnp.int32)
    used = jnp.any(head_map[:, None] == slot_ids[None, :], axis=0)
    in_use = used.astype(jnp.float32)
    used = used.astype(jnp.int32)
    place = lax.axis_index("row").reshape(1).astype(jnp.int32)
    seg_all = gather_rows(segment_ids)
    edge = jnp.sum(
        (seg_all[:, None] < segment_ids[None, :]).astype(jnp.int32), axis=0, keepdims=True
    )
    wide = []
    for layer in range(LAYERS):
        wide.append(
            (
                gather_rows(w_qkv[layer]),
                gather_rows(w_out[layer].T),
                gather_rows(w_up[layer]),
                gather_rows(w_down[layer].T),
            )
        )
    stream = inputs
    records = []
    for layer in range(LAYERS):
        wide_qkv, wide_out, wide_up, wide_down = wide[layer]
        normed, standard_one, inverse_one = norm_forward(stream, gain_one[layer], shift_one[layer])
        normed_one = normed.astype(jnp.bfloat16)
        mixed = jnp.dot(normed_one, wide_qkv, preferred_element_type=jnp.float32).astype(
            jnp.bfloat16
        )
        mixed = mixed.reshape(row_tokens, slot_count, 3 * HD)
        pairs = lax.all_gather(
            mixed[..., HD:].reshape(row_tokens, slot_count * 2 * HD), "row", axis=0, tiled=True
        )
        query = jnp.pad(mixed[..., :HD] * HD ** (-0.5), ((0, 0), (0, 0), (0, HD)))
        query = query.reshape(row_tokens, slot_count * 2 * HD)
        outputs, heads_low, log_total = attend(place, used, edge, query, pairs)
        heads_low = heads_low.reshape(slot_count * HD, row_tokens)
        middle = stream + column_sum(
            lax.dot_general(
                heads_low, wide_out, (((0,), (1,)), ((), ())), preferred_element_type=jnp.float32
            )
        )
        normed, standard_two, inverse_two = norm_forward(middle, gain_two[layer], shift_two[layer])
        normed_two = normed.astype(jnp.bfloat16)
        hidden = jnp.dot(normed_two, wide_up, preferred_element_type=jnp.float32)
        active = jax.nn.gelu(hidden, approximate=False).astype(jnp.bfloat16)
        branch = contract_cols(active, wide_down)
        if layer < LAYERS - 1:
            stream = middle + column_sum(branch)
        else:
            branch = branch.astype(jnp.bfloat16)
        records.append(
            (
                normed_one,
                standard_one,
                inverse_one,
                query,
                pairs,
                outputs,
                log_total,
                heads_low,
                standard_two,
                inverse_two,
                normed_two,
                hidden,
                active,
            )
        )
    grad = cotangent
    shares = [None] * LAYERS
    late = ()
    norm_grads = [None] * LAYERS
    for layer in reversed(range(LAYERS)):
        (
            normed_one,
            standard_one,
            inverse_one,
            query,
            pairs,
            outputs,
            log_total,
            heads_low,
            standard_two,
            inverse_two,
            normed_two,
            hidden,
            active,
        ) = records[layer]
        wide_qkv, wide_out, wide_up, wide_down = wide[layer]
        grad_low = grad.astype(jnp.bfloat16)
        grad_active = jnp.dot(grad_low, wide_down, preferred_element_type=jnp.float32)
        ignored, pullback = jax.vjp(partial(jax.nn.gelu, approximate=False), hidden)
        grad_hidden = pullback(grad_active)[0].astype(jnp.bfloat16)
        incoming = column_sum(contract_cols(grad_hidden, wide_up))
        share_down = Share(grad_low, active)
        share_up = Share(normed_two, grad_hidden)
        incoming = beside(incoming, share_down, share_up, *late)
        back_two, gain_part_two, shift_part_two = norm_backward(
            incoming, standard_two, inverse_two, gain_two[layer]
        )
        grad = grad + back_two
        grad_low = grad.astype(jnp.bfloat16)
        grad_heads = (
            jnp.dot(grad_low, wide_out, preferred_element_type=jnp.float32).reshape(
                row_tokens, slot_count, HD
            )
            * in_use[None, :, None]
        )
        grad_heads = jnp.pad(grad_heads.astype(jnp.bfloat16), ((0, 0), (0, 0), (HD, 0)))
        grad_heads = grad_heads.reshape(row_tokens, slot_count * 2 * HD)
        if layer == LAYERS - 1:
            branch, grad_heads = lax.optimization_barrier((branch, grad_heads))
            branch = lax.psum(branch, "col")
        share_out = Share(grad_low, heads_low, 1)
        grad_query, grad_pairs = attend_back(
            place, edge, query, grad_heads, pairs, outputs, log_total
        )
        if layer == LAYERS - 1:
            branch, grad_pairs = lax.optimization_barrier((branch, grad_pairs))
            output = middle + branch.astype(jnp.float32)
        grad_pairs = beside(grad_pairs, share_down, share_up, share_out, *late)
        grad_pairs = lax.psum_scatter(grad_pairs, "row", scatter_dimension=0, tiled=True)
        grad_pairs = beside(grad_pairs, share_down, share_up)
        grad_mixed = jnp.concatenate(
            [
                grad_query.reshape(row_tokens, slot_count, 2 * HD)[..., :HD],
                grad_pairs.reshape(row_tokens, slot_count, 2 * HD),
            ],
            axis=-1,
        ).reshape(row_tokens, slot_count * 3 * HD)
        incoming = column_sum(contract_cols(grad_mixed, wide_qkv))
        share_qkv = Share(normed_one, grad_mixed)
        if layer:
            incoming = beside(incoming, share_qkv, share_out)
        late = (share_qkv, share_out)
        back_one, gain_part_one, shift_part_one = norm_backward(
            incoming, standard_one, inverse_one, gain_one[layer]
        )
        grad = grad + back_one
        shares[layer] = (share_qkv, share_out, share_up, share_down)
        two = everyone_sum(jnp.stack([gain_part_two, shift_part_two]))
        one = everyone_sum(jnp.stack([gain_part_one, shift_part_one]))
        norm_grads[layer] = (one[0], one[1], two[0], two[1])
    norms = [jnp.stack(parts) for parts in zip(*norm_grads)]
    results = [[share.result() for share in group] for group in shares]
    weights = [
        jnp.stack([part.T if turned else part for part in parts])
        for parts, turned in zip(zip(*results), (False, True, False, True))
    ]
    return (output, grad, *norms, *weights)


def solution(mesh):
    placed = (
        P(("dp", "row"), None),
        P(("dp", "row")),
        P(),
        P(),
        P(),
        P(),
        P(),
        P(None, "row", "col"),
        P(None, "col", "row"),
        P(None, "row", "col"),
        P(None, "col", "row"),
        P(("dp", "row"), None),
    )
    return jax.shard_map(
        body,
        mesh=mesh,
        in_specs=placed,
        out_specs=(
            P(("dp", "row"), None),
            P(("dp", "row"), None),
            P(),
            P(),
            P(),
            P(),
            P(None, "row", "col"),
            P(None, "col", "row"),
            P(None, "row", "col"),
            P(None, "col", "row"),
        ),
        check_vma=False,
    )
```
